32 devices in a mesh: rep: 2 (over y), dp: 16 (over z, x, core), tensor: 1.
Axes of the slice: x: 2, y: 2, z: 4, core: 2. Of those that a mesh axis runs over, the one named last changes fastest.
Arguments:
- tokens: bfloat16 [16384, 8192], P(('rep', 'dp'), 'tensor'), parts along dimension 0, may hold values from -6 to 6
- value_weight: bfloat16 [8192, 1024], P('tensor'), may hold values from -0.0625 to 0.0625
- adapter_down_weight: bfloat16 [8192, 16384], P('tensor', 'dp'), may hold values from -0.0625 to 0.0625
- adapter_up_weight: bfloat16 [16384, 1024], P('dp', 'tensor'), may hold values from -0.5 to 0.5
- row_adapter_index: int32 [16384], P(('rep', 'dp')), parts along dimension 0, may hold values from 0 to 255, as said below
- placement: int32 [512], P('rep'), parts along dimension 0, may hold values from 0 to 255, as said below
Outputs:
- values_out: bfloat16 [16384, 1024], P(('rep', 'dp'), 'tensor'), parts along dimension 0
The draws below stay inside these ranges and needn't reach their ends.
There are 2 independent parts, one for each index of `rep`. The reference program is written for one: setup_inputs(seed, part) draws one part's arguments, and reference() takes and returns one part's arrays. A program takes and returns all parts, laid end to end along the dimension named above; an argument that names none is the same for every part. Nothing has to cross between parts.
Inputs may be any that keep to these rules, and one draw needn't show every extreme that they name: `row_adapter_index`: the owner group of adapter a is placement[a] // 16. The rows of one index of dp name adapters of one owner group at most 64 times; in every draw one owner group, the same for every index of dp, is named exactly 64 times by the rows of every index of dp. `placement`: A permutation of the adapters over the slots.
All inputs are finite; a program needn't handle non-finite values.
Results may differ from the reference program's by a relative error of at most 0.0042.
Values may be sent and summed in bfloat16 or wider, within the bound.
A program may use at most 128 MiB of HBM per device.

```python
import jax
import jax.numpy as jnp
from jax import lax

MODEL_WIDTH = 8192
VALUE_WIDTH = 1024
ADAPTER_RANK = 64
ADP_DEV = 16
ROWS = 512
ADAPTER_COUNT = 256
ROWS_T = 8192
CAP = 64
N_DP = 16


def slot_owners(key):
    return jax.random.permutation(jax.random.fold_in(key, 11), ADAPTER_COUNT).astype(jnp.int32)


def draw_placement(key, part):
    inverse = slot_owners(key)
    return jnp.argsort(inverse, stable=True).astype(jnp.int32)


def draw_row_adapter_index(key, part):
    inverse = slot_owners(key)
    key = jax.random.fold_in(key, 5)
    key_hot, key_weight, key_order, key_local = jax.random.split(key, 4)
    hottest = jax.random.randint(key_hot, (), 0, N_DP).astype(jnp.int32)
    weights = jax.random.randint(key_weight, (N_DP, N_DP - 1), 2, 4).astype(jnp.int32)
    running = jnp.cumsum(weights, axis=1).astype(jnp.int32)
    total = running[:, -1:]
    bounds = (ROWS - CAP) * running // total
    offsets = (jnp.arange(ROWS, dtype=jnp.int32) - CAP)[None, :]
    ranked = jnp.sum((bounds[:, None, :] <= offsets[:, :, None]).astype(jnp.int32), axis=2)
    others = (hottest + 1 + ranked) % N_DP
    owners = jnp.where(jnp.arange(ROWS, dtype=jnp.int32)[None, :] < CAP, hottest, others).astype(jnp.int32)
    orders = jax.vmap(lambda one_key: jax.random.permutation(one_key, ROWS))(jax.random.split(key_order, N_DP))
    owners = jnp.take_along_axis(owners, orders.astype(jnp.int32), axis=1)
    local = jax.random.randint(key_local, (N_DP, ROWS), 0, ADP_DEV).astype(jnp.int32)
    chosen = inverse[owners * ADP_DEV + local]
    return chosen.reshape(ROWS_T).astype(jnp.int32)


def steps_of(key, extent, pieces, least, largest):
    loudness, own = 1.0, jax.random.fold_in(key, 6)
    for dim, parts in pieces:
        steps = jnp.exp(jax.random.uniform(jax.random.fold_in(own, dim), (parts,), jnp.float32, least / len(pieces), largest / len(pieces)))
        loudness = loudness * jnp.repeat(steps, extent[dim] // parts).reshape([-1 if axis == dim else 1 for axis in range(len(extent))])
    return loudness


def scatter_about(key, dims, width, reach, cuts=(), held_as=jnp.bfloat16):
    entries = width * jax.random.normal(key, dims, jnp.float32)
    if cuts:
        entries = entries * steps_of(key, dims, cuts, -0.22, 0.18)
    return jnp.clip(entries, -reach, reach).astype(held_as)


def setup_inputs(seed: int = 0, part: int = 0) -> dict:
    streams_of = jax.random.split(jax.random.key(seed), 7)
    own_keys = jax.random.split(jax.random.fold_in(streams_of[6], part), 7)
    return {
        "tokens": scatter_about(own_keys[0], (ROWS_T, MODEL_WIDTH), 1.0, 6.0, ((0, 16),)),
        "value_weight": scatter_about(streams_of[1], (MODEL_WIDTH, VALUE_WIDTH), MODEL_WIDTH ** -0.5, 0.0625),
        "adapter_down_weight": scatter_about(streams_of[2], (MODEL_WIDTH, ADAPTER_COUNT * ADAPTER_RANK), MODEL_WIDTH ** -0.5, 0.0625, ((1, 16),)),
        "adapter_up_weight": scatter_about(streams_of[3], (ADAPTER_COUNT * ADAPTER_RANK, VALUE_WIDTH), 0.08, 0.5, ((0, 16),)),
        "row_adapter_index": draw_row_adapter_index(jax.random.fold_in(jax.random.fold_in(streams_of[6], part), 71), part),
        "placement": draw_placement(jax.random.fold_in(jax.random.fold_in(streams_of[6], part), 71), part),
    }


def reference(tokens, value_weight, adapter_down_weight, adapter_up_weight, row_adapter_index, placement):
    base = jnp.dot(tokens, value_weight, preferred_element_type=jnp.float32)
    slots = placement[row_adapter_index].astype(jnp.int32)
    down_matrices = adapter_down_weight.reshape(MODEL_WIDTH, ADAPTER_COUNT, ADAPTER_RANK)
    up_matrices = adapter_up_weight.reshape(ADAPTER_COUNT, ADAPTER_RANK, VALUE_WIDTH)

    def one_block(pair):
        block_rows, block_slots = pair
        picked = jnp.take(down_matrices, block_slots, axis=1)
        low = jnp.einsum("bd,dbr->br", block_rows.astype(jnp.float32), picked.astype(jnp.float32))
        low = low.astype(jnp.bfloat16)
        ups = jnp.take(up_matrices, block_slots, axis=0)
        adapter_update = jnp.einsum("br,brk->bk", low.astype(jnp.float32), ups.astype(jnp.float32))
        return adapter_update.astype(jnp.bfloat16)

    deltas = lax.map(one_block, (tokens.reshape(ROWS_T // 128, 128, MODEL_WIDTH), slots.reshape(ROWS_T // 128, 128)))
    deltas = deltas.reshape(ROWS_T, VALUE_WIDTH)
    return (base + deltas.astype(jnp.float32)).astype(jnp.bfloat16)
```

```python
import jax
import jax.numpy as jnp
from jax import lax
from jax.sharding import PartitionSpec as P

ADAPTER_RANK = 64


def owner_task(rows, tags, first_slot, down, up):
    columns = lax.broadcasted_iota(jnp.int32, (1, down.shape[1]), 1) // ADAPTER_RANK
    mask = (tags.reshape(-1, 1) - 1 - first_slot) == columns
    part = jnp.dot(rows, down, preferred_element_type=jnp.float32)
    part = jnp.where(mask, part, 0.0)
    if lax.axis_size("tensor") > 1:
        folded = jnp.sum(part.reshape(part.shape[0], -1, ADAPTER_RANK), axis=1)
        folded = lax.psum(folded, "tensor")
        part = jnp.where(mask, jnp.tile(folded, (1, down.shape[1] // ADAPTER_RANK)), 0.0)
    return jnp.dot(
        part.astype(jnp.bfloat16), up, preferred_element_type=jnp.float32
    ).astype(jnp.bfloat16)


def plan(row_adapter_index, placement, groups, resident, share):
    rows = row_adapter_index.shape[0]
    adapters = jnp.arange(placement.shape[0], dtype=jnp.int32)
    slots = jnp.sum(
        jnp.where(row_adapter_index[:, None] == adapters[None, :], placement[None, :], 0), axis=1
    )
    owners = slots // resident
    onehot = owners[:, None] == jnp.arange(groups, dtype=jnp.int32)[None, :]
    order = jnp.arange(rows, dtype=jnp.int32)
    before = (order[:, None] > order[None, :]).astype(jnp.bfloat16)
    ranks = jnp.dot(before, onehot.astype(jnp.bfloat16), preferred_element_type=jnp.float32)
    position = jnp.sum(jnp.where(onehot, ranks, 0.0), axis=1).astype(jnp.int32)
    over = jnp.maximum(jnp.sum(onehot.astype(jnp.int32), axis=0) - share, 0)
    group = jnp.arange(groups, dtype=jnp.int32)
    offset = jnp.sum(jnp.where(group[None, :] < group[:, None], over[None, :], 0), axis=1)
    row_offset = jnp.sum(jnp.where(onehot, offset[None, :], 0), axis=1)
    place = jnp.where(
        position < share,
        owners * share + position,
        groups * share + row_offset + position - share,
    )
    return slots, place, jnp.sum(over)


def per_device(
    tokens, value_weight, adapter_down_weight, adapter_up_weight, row_adapter_index, placement
):
    rows, width = tokens.shape
    groups = lax.axis_size("dp")
    me = lax.axis_index("dp")
    resident = adapter_down_weight.shape[1] // ADAPTER_RANK
    share = rows // groups
    spill = rows * 5 // 32
    direct = groups * share
    first_slot = me * resident
    slots, place, over = plan(row_adapter_index, placement, groups, resident, share)
    most = lax.pmax(over, ("rep", "dp", "tensor"))

    def pick(start, count):
        return (start + jnp.arange(count, dtype=jnp.int32))[:, None] == place[None, :]

    def packed(chosen):
        return jnp.dot(
            chosen.astype(jnp.bfloat16), tokens, preferred_element_type=jnp.float32
        ).astype(jnp.bfloat16)

    def tagged(chosen):
        return jnp.sum(jnp.where(chosen, slots[None, :] + 1, 0), axis=1)

    def spilled(start):
        chosen = pick(start, spill)
        gathered = lax.all_gather(packed(chosen), "dp", tiled=True)
        tags = lax.all_gather(tagged(chosen), "dp", tiled=True)
        delta = owner_task(gathered, tags, first_slot, adapter_down_weight, adapter_up_weight)
        return lax.psum_scatter(delta, "dp", scatter_dimension=0, tiled=True)

    def unpacked(start, returned):
        chosen = pick(start, returned.shape[0])
        return lax.dot_general(
            chosen.astype(jnp.bfloat16),
            returned,
            (((0,), (0,)), ((), ())),
            preferred_element_type=jnp.float32,
        )

    spill_back = spilled(direct)
    chosen = pick(0, direct)
    sent = packed(chosen).reshape(groups, share, width)
    tags = lax.all_to_all(tagged(chosen).reshape(groups, share), "dp", 0, 0, tiled=True)
    received = lax.all_to_all(sent, "dp", 0, 0, tiled=True).reshape(direct, width)
    base = lax.psum_scatter(
        jnp.dot(tokens, value_weight, preferred_element_type=jnp.float32),
        "tensor",
        scatter_dimension=1,
        tiled=True,
    )
    delta = owner_task(received, tags, first_slot, adapter_down_weight, adapter_up_weight)
    back = lax.all_to_all(
        delta.reshape(groups, share, -1), "dp", 0, 0, tiled=True
    ).reshape(direct, -1)
    row_delta = unpacked(0, back) + unpacked(direct, spill_back)

    def more(state):
        return state[0] < most

    def again(state):
        done, total = state
        return done + spill, total + unpacked(direct + done, spilled(direct + done))

    row_delta = lax.while_loop(more, again, (jnp.int32(spill), row_delta))[1]
    return (base + row_delta).astype(jnp.bfloat16)


def solution(mesh):
    placed = (
        P(("rep", "dp"), "tensor"),
        P("tensor", None),
        P("tensor", "dp"),
        P("dp", "tensor"),
        P(("rep", "dp")),
        P("rep"),
    )
    return jax.shard_map(
        per_device,
        mesh=mesh,
        in_specs=placed,
        out_specs=P(("rep", "dp"), "tensor"),
        check_vma=False,
    )
```

```python
import functools

import jax
import jax.numpy as jnp
from jax import lax
from jax.experimental import pallas as pl
from jax.experimental.pallas import tpu as pltpu
from jax.sharding import PartitionSpec as P

ADAPTER_RANK = 64


MESH = pl.DeviceIdType.MESH
TILE = 256


def flipped(a, b, bits):
    return sum(((a // 2**j + b // 2**j) % 2) * 2**j for j in range(bits))


def mirrored(a, bits):
    return sum(((a // 2**j) % 2) * 2 ** (bits - 1 - j) for j in range(bits))


def exchange_kernel(
    bits,
    x_hbm,
    y_hbm,
    down_hbm,
    up_hbm,
    tag_ref,
    spill_tag_ref,
    back,
    spill_back,
    down,
    up,
    received,
    gathered,
    delta,
    spill_delta,
    halves,
    low,
    spill_low,
    own_sem,
    sent_sem,
    came_sem,
    back_sent,
    back_came,
    gather_sent,
    gather_came,
    halve_sent,
    halve_came,
):
    n = 2**bits
    rep, me = lax.axis_index("rep"), lax.axis_index("dp")
    place = mirrored(me, bits)
    spill = gathered.shape[1]
    width = down.shape[1]
    group = max(1, 128 // spill)

    barrier = pltpu.get_barrier_semaphore()

    def greet(k, _):
        pl.semaphore_signal(
            barrier, inc=1, device_id=(rep, flipped(me, k, bits), 0), device_id_type=MESH
        )
        return 0

    lax.fori_loop(1, n, greet, 0)
    pl.semaphore_wait(barrier, n - 1)

    own_spill = pltpu.make_async_copy(y_hbm, gathered.at[place], own_sem.at[0])
    own_rows = pltpu.make_async_copy(x_hbm.at[me], received.at[me], own_sem.at[1])
    own_down = pltpu.make_async_copy(down_hbm, down, own_sem.at[2])
    own_up = pltpu.make_async_copy(up_hbm, up, own_sem.at[3])
    own_back = pltpu.make_async_copy(delta.at[me], back.at[me], own_sem.at[4])
    own_spill_back = pltpu.make_async_copy(spill_delta.at[place], spill_back, own_sem.at[5])

    def forward(k):
        d = flipped(me, k, bits)
        return pltpu.make_async_remote_copy(
            src_ref=x_hbm.at[d],
            dst_ref=received.at[me],
            send_sem=sent_sem.at[k],
            recv_sem=came_sem.at[k],
            device_id=(rep, d, 0),
            device_id_type=MESH,
        )

    def backward(k):
        d = flipped(me, k, bits)
        return pltpu.make_async_remote_copy(
            src_ref=delta.at[d],
            dst_ref=back.at[me],
            send_sem=back_sent.at[k],
            recv_sem=back_came.at[k],
            device_id=(rep, d, 0),
            device_id_type=MESH,
        )

    def gather(t):
        h = 2**t
        blocks = pl.ds(place // h * h, h)
        return pltpu.make_async_remote_copy(
            src_ref=gathered.at[blocks],
            dst_ref=gathered.at[blocks],
            send_sem=gather_sent.at[t],
            recv_sem=gather_came.at[t],
            device_id=(rep, flipped(me, n // 2 // h, bits), 0),
            device_id_type=MESH,
        )

    def halve(t):
        h = n // 2 // 2**t
        mine = place // h * h
        other = place // (2 * h) * (4 * h) + h - mine
        return pltpu.make_async_remote_copy(
            src_ref=spill_delta.at[pl.ds(other, h)],
            dst_ref=halves.at[pl.ds(n - 2 * h, h)],
            send_sem=halve_sent.at[t],
            recv_sem=halve_came.at[t],
            device_id=(rep, flipped(me, 2**t, bits), 0),
            device_id_type=MESH,
        )

    def halved(t):
        h = n // 2 // 2**t
        halve(t).wait_recv()
        mine = pl.ds(place // h * h, h)
        spill_delta[mine] = spill_delta[mine] + halves[pl.ds(n - 2 * h, h)]

    def projected(rows, tags, low_ref):
        def tile(c, _):
            columns = pl.ds(pl.multiple_of(c * TILE, TILE), TILE)
            part = jnp.dot(rows(), down[:, columns], preferred_element_type=jnp.float32)
            slot = (
                lax.broadcasted_iota(jnp.int32, (1, TILE), 1) + c * TILE
            ) // ADAPTER_RANK
            low_ref[:, columns] = jnp.where(tags == slot, part, 0.0).astype(jnp.bfloat16)
            return 0

        lax.fori_loop(0, width // TILE, tile, 0)
        return jnp.dot(low_ref[...], up[...], preferred_element_type=jnp.float32).astype(
            jnp.bfloat16
        )

    def process(source):
        delta[source] = projected(lambda: received[source], tag_ref[source][:, :1], low)

    def process_spill():
        def some(q, _):
            blocks = pl.ds(q * group, group)
            rows = group * spill
            out = projected(
                lambda: gathered[blocks].reshape(rows, gathered.shape[2]),
                spill_tag_ref[blocks].reshape(rows, 128)[:, :1],
                spill_low,
            )
            spill_delta[blocks] = out.reshape(group, spill, out.shape[1])
            return 0

        lax.fori_loop(0, n // group, some, 0)

    def turn(j):
        return (1 - j % 2) * (n // 2 + j // 2) + (j % 2) * ((j + 1) // 2)

    own_spill.start()
    own_rows.start()
    own_spill.wait()
    gather(0).start()
    window = 4

    def begin(j, _):
        forward(turn(j)).start()
        return 0

    lax.fori_loop(0, window, begin, 0)
    own_down.start()
    own_up.start()
    own_rows.wait()
    own_down.wait()
    own_up.wait()
    process(me)
    own_back.start()

    def step(j, _):
        k = turn(j)
        forward(k).wait_send()

        @pl.when(j + window < n - 1)
        def _():
            forward(turn(j + window)).start()

        for t in range(bits - 1):

            @pl.when(j == t + 1)
            def _(t=t):
                gather(t).wait_recv()
                gather(t + 1).start()

        @pl.when(j == bits + 2)
        def _():
            gather(bits - 1).wait_recv()
            process_spill()
            halve(0).start()

        for t in range(bits):

            @pl.when(j == bits + 3 + t)
            def _(t=t):
                halved(t)
                if t + 1 < bits:
                    halve(t + 1).start()
                else:
                    own_spill_back.start()

        forward(k).wait_recv()
        process(flipped(me, k, bits))
        backward(k).start()
        return 0

    lax.fori_loop(0, n - 1, step, 0)

    def finish(k, _):
        backward(k).wait_send()
        backward(k).wait_recv()
        return 0

    for t in range(bits):
        gather(t).wait_send()
        halve(t).wait_send()
    lax.fori_loop(1, n, finish, 0)
    own_back.wait()
    own_spill_back.wait()


def exchange(x, y, down, up, tags, spill_tags):
    n, share, width = x.shape
    spill = y.shape[0]
    bits = n.bit_length() - 1
    columns, outs = down.shape[1], up.shape[1]
    group = max(1, 128 // spill)
    anywhere, vmem = pl.BlockSpec(memory_space=pl.ANY), pl.BlockSpec(memory_space=pltpu.VMEM)
    work = 2 * (n * share + n * spill) * (width * columns + columns * outs)
    return pl.pallas_call(
        functools.partial(exchange_kernel, bits),
        out_shape=(
            jax.ShapeDtypeStruct((n, share, outs), jnp.bfloat16),
            jax.ShapeDtypeStruct((spill, outs), jnp.bfloat16),
        ),
        in_specs=[anywhere] * 4 + [vmem] * 2,
        out_specs=(anywhere, anywhere),
        scratch_shapes=[
            pltpu.VMEM((width, columns), jnp.bfloat16),
            pltpu.VMEM((columns, outs), jnp.bfloat16),
            pltpu.VMEM((n, share, width), jnp.bfloat16),
            pltpu.VMEM((n, spill, width), jnp.bfloat16),
            pltpu.VMEM((n, share, outs), jnp.bfloat16),
            pltpu.VMEM((n, spill, outs), jnp.bfloat16),
            pltpu.VMEM((n - 1, spill, outs), jnp.bfloat16),
            pltpu.VMEM((share, columns), jnp.bfloat16),
            pltpu.VMEM((group * spill, columns), jnp.bfloat16),
            pltpu.SemaphoreType.DMA((6,)),
        ]
        + [pltpu.SemaphoreType.DMA((n,))] * 4
        + [pltpu.SemaphoreType.DMA((bits,))] * 4,
        compiler_params=pltpu.CompilerParams(
            collective_id=0, has_side_effects=True, vmem_limit_bytes=56 * 2**20
        ),
        cost_estimate=pl.CostEstimate(flops=work, bytes_accessed=2**25, transcendentals=0),
    )(x, y, down, up, tags, spill_tags)


def owner_task(rows, tags, first_slot, down, up):
    columns = lax.broadcasted_iota(jnp.int32, (1, down.shape[1]), 1) // ADAPTER_RANK
    mask = (tags.reshape(-1, 1) - 1 - first_slot) == columns
    part = jnp.dot(rows, down, preferred_element_type=jnp.float32)
    part = jnp.where(mask, part, 0.0)
    if lax.axis_size("tensor") > 1:
        folded = jnp.sum(part.reshape(part.shape[0], -1, ADAPTER_RANK), axis=1)
        folded = lax.psum(folded, "tensor")
        part = jnp.where(mask, jnp.tile(folded, (1, down.shape[1] // ADAPTER_RANK)), 0.0)
    return jnp.dot(
        part.astype(jnp.bfloat16), up, preferred_element_type=jnp.float32
    ).astype(jnp.bfloat16)


def plan(row_adapter_index, placement, groups, resident, shares):
    rows = row_adapter_index.shape[0]
    adapters = jnp.arange(placement.shape[0], dtype=jnp.int32)
    slots = jnp.sum(
        jnp.where(row_adapter_index[:, None] == adapters[None, :], placement[None, :], 0), axis=1
    )
    owners = slots // resident
    onehot = owners[:, None] == jnp.arange(groups, dtype=jnp.int32)[None, :]
    order = jnp.arange(rows, dtype=jnp.int32)
    before = (order[:, None] > order[None, :]).astype(jnp.bfloat16)
    ranks = jnp.dot(before, onehot.astype(jnp.bfloat16), preferred_element_type=jnp.float32)
    position = jnp.sum(jnp.where(onehot, ranks, 0.0), axis=1).astype(jnp.int32)
    over = jnp.maximum(jnp.sum(onehot.astype(jnp.int32), axis=0) - sum(shares), 0)
    group = jnp.arange(groups, dtype=jnp.int32)
    offset = jnp.sum(jnp.where(group[None, :] < group[:, None], over[None, :], 0), axis=1)
    place = jnp.sum(jnp.where(onehot, offset[None, :], 0), axis=1)
    place = place + position + (groups - 1) * sum(shares)
    end = sum(shares)
    for share in reversed(shares):
        start = end - share
        place = jnp.where(
            position < end, groups * start + owners * share + position - start, place
        )
        end = start
    return slots, place, jnp.sum(over)


def per_device(
    tokens, value_weight, adapter_down_weight, adapter_up_weight, row_adapter_index, placement
):
    rows, width = tokens.shape
    groups, copies = lax.axis_size("dp"), lax.axis_size("rep")
    me = lax.axis_index("dp")
    resident = adapter_down_weight.shape[1] // ADAPTER_RANK
    whole = rows * 5 // (4 * groups)
    fused = lax.axis_size("tensor") == 1 and groups >= 16 and groups & (groups - 1) == 0
    shares = (whole,) if fused else (whole * 3 // 5, whole - whole * 3 // 5)
    spill = rows // 16
    direct = groups * whole
    first_slot = me * resident
    slots, place, over = plan(row_adapter_index, placement, groups, resident, shares)

    def pick(start, count):
        return (start + jnp.arange(count, dtype=jnp.int32))[:, None] == place[None, :]

    def packed(start, count):
        return jnp.dot(
            pick(start, count).astype(jnp.bfloat16), tokens, preferred_element_type=jnp.float32
        ).astype(jnp.bfloat16)

    def tagged(start, count):
        return jnp.sum(jnp.where(pick(start, count), slots[None, :] + 1, 0), axis=1)

    def owned(received, tags):
        return owner_task(received, tags, first_slot, adapter_down_weight, adapter_up_weight)

    def gathered(start):
        return lax.all_gather(packed(start, spill), "dp", tiled=True)

    def scattered(delta):
        return lax.psum_scatter(delta, "dp", scatter_dimension=0, tiled=True)

    def unpacked(start, returned):
        return lax.dot_general(
            pick(start, returned.shape[0]).astype(jnp.bfloat16),
            returned,
            (((0,), (0,)), ((), ())),
            preferred_element_type=jnp.float32,
        )

    starts = (0, groups * shares[0])[: len(shares)]
    notes = jnp.concatenate(
        [tagged(start, groups * share).reshape(groups, share) for start, share in zip(starts, shares)]
        + [
            jnp.broadcast_to(tagged(direct, spill)[None, :], (groups, spill)),
            jnp.broadcast_to(over, (groups, 1)),
        ],
        axis=1,
    )
    notes = lax.all_to_all(jnp.tile(notes, (copies, 1)), ("rep", "dp"), 0, 0, tiled=True)
    most = jnp.max(notes[:, -1])
    notes = lax.dynamic_slice_in_dim(notes, lax.axis_index("rep") * groups, groups, 0)

    base = lax.psum_scatter(
        jnp.dot(tokens, value_weight, preferred_element_type=jnp.float32),
        "tensor",
        scatter_dimension=1,
        tiled=True,
    )
    if fused:
        bits = groups.bit_length() - 1
        mirror = [mirrored(s, bits) for s in range(groups)]
        local = notes[:, : whole + spill] - 1 - first_slot
        spill_local = jnp.stack([local[s, whole:] for s in mirror])
        back, spill_back = exchange(
            packed(0, direct).reshape(groups, whole, width),
            packed(direct, spill),
            adapter_down_weight,
            adapter_up_weight,
            jnp.broadcast_to(local[:, :whole, None], (groups, whole, 128)),
            jnp.broadcast_to(spill_local[:, :, None], (groups, spill, 128)),
        )
        backs = [back.reshape(direct, -1)]
    else:
        spilled = gathered(direct)
        arrived = [
            lax.all_to_all(
                packed(start, groups * share).reshape(groups, share, width), "dp", 0, 0, tiled=True
            ).reshape(groups * share, width)
            for start, share in zip(starts, shares)
        ]
        base, spilled = lax.optimization_barrier((base, spilled))
        spill_back = scattered(owned(spilled, notes[:, whole : whole + spill]))
        backs = []
        for at, share, block in zip((0, shares[0]), shares, arrived):
            delta = owned(block, notes[:, at : at + share])
            backs.append(
                lax.all_to_all(delta.reshape(groups, share, -1), "dp", 0, 0, tiled=True).reshape(
                    groups * share, -1
                )
            )
    row_delta = unpacked(0, jnp.concatenate(backs + [spill_back], axis=0))

    def more(state):
        return state[0] < most

    def again(state):
        done, total = state
        tags = lax.all_gather(tagged(direct + done, spill), "dp", tiled=True)
        back = scattered(owned(gathered(direct + done), tags))
        return done + spill, total + unpacked(direct + done, back)

    row_delta = lax.while_loop(more, again, (jnp.int32(spill), row_delta))[1]
    return (base + row_delta).astype(jnp.bfloat16)


def solution(mesh):
    placed = (
        P(("rep", "dp"), "tensor"),
        P("tensor", None),
        P("tensor", "dp"),
        P("dp", "tensor"),
        P(("rep", "dp")),
        P("rep"),
    )
    return jax.shard_map(
        per_device,
        mesh=mesh,
        in_specs=placed,
        out_specs=P(("rep", "dp"), "tensor"),
        check_vma=False,
    )
```

```python
import functools

import jax
import jax.numpy as jnp
from jax import lax
from jax.experimental import pallas as pl
from jax.experimental.pallas import tpu as pltpu
from jax.sharding import PartitionSpec as P

ADAPTER_RANK = 64


MESH = pl.DeviceIdType.MESH
TILE = 256
WINDOW = 4
GAP = 3


def flipped(a, b, bits):
    return sum(((a // 2**j + b // 2**j) % 2) * 2**j for j in range(bits))


def mirrored(a, bits):
    return sum(((a // 2**j) % 2) * 2 ** (bits - 1 - j) for j in range(bits))


def exchange_kernel(
    bits,
    x_hbm,
    y_hbm,
    down_hbm,
    up_hbm,
    tokens_hbm,
    value_hbm,
    tag_ref,
    spill_tag_ref,
    back,
    spill_back,
    base_out,
    down,
    up,
    received,
    gathered,
    delta,
    spill_delta,
    halves,
    low,
    spill_low,
    token_part,
    value_part,
    base,
    base_sem,
    own_sem,
    sent_sem,
    came_sem,
    back_sent,
    back_came,
    gather_sent,
    gather_came,
    halve_sent,
    halve_came,
):
    n = 2**bits
    rep, me = lax.axis_index("rep"), lax.axis_index("dp")
    place = mirrored(me, bits)
    spill = gathered.shape[1]
    width = down.shape[1]
    group = max(1, 128 // spill)

    barrier = pltpu.get_barrier_semaphore()

    def greet(k, _):
        pl.semaphore_signal(
            barrier, inc=1, device_id=(rep, flipped(me, k, bits), 0), device_id_type=MESH
        )
        return 0

    lax.fori_loop(1, n, greet, 0)
    pl.semaphore_wait(barrier, n - 1)

    own_spill = pltpu.make_async_copy(y_hbm, gathered.at[place], own_sem.at[0])
    own_rows = pltpu.make_async_copy(x_hbm.at[me], received.at[me], own_sem.at[1])
    own_down = pltpu.make_async_copy(down_hbm, down, own_sem.at[2])
    own_up = pltpu.make_async_copy(up_hbm, up, own_sem.at[3])
    own_back = pltpu.make_async_copy(delta.at[me], back.at[me], own_sem.at[4])
    own_spill_back = pltpu.make_async_copy(spill_delta.at[place], spill_back, own_sem.at[5])

    def forward(k):
        d = flipped(me, k, bits)
        return pltpu.make_async_remote_copy(
            src_ref=x_hbm.at[d],
            dst_ref=received.at[me],
            send_sem=sent_sem.at[k],
            recv_sem=came_sem.at[k],
            device_id=(rep, d, 0),
            device_id_type=MESH,
        )

    def backward(k):
        d = flipped(me, k, bits)
        return pltpu.make_async_remote_copy(
            src_ref=delta.at[d],
            dst_ref=back.at[me],
            send_sem=back_sent.at[k],
            recv_sem=back_came.at[k],
            device_id=(rep, d, 0),
            device_id_type=MESH,
        )

    def gather(t):
        h = 2**t
        blocks = pl.ds(place // h * h, h)
        return pltpu.make_async_remote_copy(
            src_ref=gathered.at[blocks],
            dst_ref=gathered.at[blocks],
            send_sem=gather_sent.at[t],
            recv_sem=gather_came.at[t],
            device_id=(rep, flipped(me, n // 2 // h, bits), 0),
            device_id_type=MESH,
        )

    def halve(t):
        h = n // 2 // 2**t
        mine = place // h * h
        other = place // (2 * h) * (4 * h) + h - mine
        return pltpu.make_async_remote_copy(
            src_ref=spill_delta.at[pl.ds(other, h)],
            dst_ref=halves.at[pl.ds(n - 2 * h, h)],
            send_sem=halve_sent.at[t],
            recv_sem=halve_came.at[t],
            device_id=(rep, flipped(me, 2**t, bits), 0),
            device_id_type=MESH,
        )

    def halved(t):
        h = n // 2 // 2**t
        halve(t).wait_recv()
        mine = pl.ds(place // h * h, h)
        spill_delta[mine] = spill_delta[mine] + halves[pl.ds(n - 2 * h, h)]

    def projected(rows, tags, low_ref):
        def tile(c, _):
            columns = pl.ds(pl.multiple_of(c * TILE, TILE), TILE)
            part = jnp.dot(rows(), down[:, columns], preferred_element_type=jnp.float32)
            slot = (
                lax.broadcasted_iota(jnp.int32, (1, TILE), 1) + c * TILE
            ) // ADAPTER_RANK
            low_ref[:, columns] = jnp.where(tags == slot, part, 0.0).astype(jnp.bfloat16)
            return 0

        lax.fori_loop(0, width // TILE, tile, 0)
        return jnp.dot(low_ref[...], up[...], preferred_element_type=jnp.float32).astype(
            jnp.bfloat16
        )

    def process(source):
        delta[source] = projected(lambda: received[source], tag_ref[source][:, :1], low)

    def process_spill():
        def some(q, _):
            blocks = pl.ds(q * group, group)
            rows = group * spill
            out = projected(
                lambda: gathered[blocks].reshape(rows, gathered.shape[2]),
                spill_tag_ref[blocks].reshape(rows, 128)[:, :1],
                spill_low,
            )
            spill_delta[blocks] = out.reshape(group, spill, out.shape[1])
            return 0

        lax.fori_loop(0, n // group, some, 0)

    def parts(c):
        slot, step_size = c % 2, token_part.shape[2]
        span = pl.ds(pl.multiple_of(c * step_size, step_size), step_size)
        return (
            pltpu.make_async_copy(
                tokens_hbm.at[:, span], token_part.at[slot], base_sem.at[2 * slot]
            ),
            pltpu.make_async_copy(
                value_hbm.at[span], value_part.at[slot], base_sem.at[2 * slot + 1]
            ),
        )

    def add_base(c):
        @pl.when(c + 1 < n)
        def _():
            for copy in parts(c + 1):
                copy.start()

        for copy in parts(c):
            copy.wait()

        def tile(t, _):
            columns = pl.ds(pl.multiple_of(t * TILE, TILE), TILE)
            base[:, columns] += jnp.dot(
                token_part[c % 2],
                value_part[c % 2, :, columns],
                preferred_element_type=jnp.float32,
            )
            return 0

        lax.fori_loop(0, base.shape[1] // TILE, tile, 0)

    def turn(j):
        return (1 - j % 2) * (n // 2 + j // 2) + (j % 2) * ((j + 1) // 2)

    own_spill.start()
    own_rows.start()
    own_spill.wait()
    gather(0).start()
    window = WINDOW

    def begin(j, _):
        forward(turn(j)).start()
        return 0

    lax.fori_loop(0, window, begin, 0)
    own_down.start()
    own_up.start()
    for copy in parts(0):
        copy.start()
    base[...] = jnp.zeros_like(base)
    own_rows.wait()
    own_down.wait()
    own_up.wait()
    process(me)
    own_back.start()
    add_base(0)

    spill_turn = GAP * (bits - 1) + 2

    def merge(t):
        halved(t)
        if t + 1 < bits:
            halve(t + 1).start()
        else:
            own_spill_back.start()

    def step(j, _):
        k = turn(j)
        add_base(j + 1)
        forward(k).wait_send()

        @pl.when(j + window < n - 1)
        def _():
            forward(turn(j + window)).start()

        forward(k).wait_recv()
        process(flipped(me, k, bits))
        backward(k).start()

        for t in range(bits - 1):

            @pl.when(j == GAP * t + 2)
            def _(t=t):
                gather(t).wait_recv()
                gather(t + 1).start()

        @pl.when(j == spill_turn)
        def _():
            gather(bits - 1).wait_recv()
            process_spill()
            halve(0).start()

        for t in range(bits):
            if spill_turn + 1 + t < n - 1:

                @pl.when(j == spill_turn + 1 + t)
                def _(t=t):
                    merge(t)

        return 0

    lax.fori_loop(0, n - 1, step, 0)
    for t in range(bits):
        if spill_turn + 1 + t >= n - 1:
            merge(t)
    own_base = pltpu.make_async_copy(base, base_out, own_sem.at[6])
    own_base.start()

    def finish(k, _):
        backward(k).wait_send()
        backward(k).wait_recv()
        return 0

    for t in range(bits):
        gather(t).wait_send()
        halve(t).wait_send()
    lax.fori_loop(1, n, finish, 0)
    own_back.wait()
    own_spill_back.wait()
    own_base.wait()


def exchange(x, y, down, up, tokens, value, tags, spill_tags):
    n, share, width = x.shape
    spill = y.shape[0]
    bits = n.bit_length() - 1
    columns, outs = down.shape[1], up.shape[1]
    group = max(1, 128 // spill)
    anywhere, vmem = pl.BlockSpec(memory_space=pl.ANY), pl.BlockSpec(memory_space=pltpu.VMEM)
    work = 2 * (n * share + n * spill) * (width * columns + columns * outs)
    return pl.pallas_call(
        functools.partial(exchange_kernel, bits),
        out_shape=(
            jax.ShapeDtypeStruct((n, share, outs), jnp.bfloat16),
            jax.ShapeDtypeStruct((spill, outs), jnp.bfloat16),
            jax.ShapeDtypeStruct((tokens.shape[0], outs), jnp.float32),
        ),
        in_specs=[anywhere] * 6 + [vmem] * 2,
        out_specs=(anywhere, anywhere, anywhere),
        scratch_shapes=[
            pltpu.VMEM((width, columns), jnp.bfloat16),
            pltpu.VMEM((columns, outs), jnp.bfloat16),
            pltpu.VMEM((n, share, width), jnp.bfloat16),
            pltpu.VMEM((n, spill, width), jnp.bfloat16),
            pltpu.VMEM((n, share, outs), jnp.bfloat16),
            pltpu.VMEM((n, spill, outs), jnp.bfloat16),
            pltpu.VMEM((n - 1, spill, outs), jnp.bfloat16),
            pltpu.VMEM((share, columns), jnp.bfloat16),
            pltpu.VMEM((group * spill, columns), jnp.bfloat16),
            pltpu.VMEM((2, tokens.shape[0], width // n), jnp.bfloat16),
            pltpu.VMEM((2, width // n, outs), jnp.bfloat16),
            pltpu.VMEM((tokens.shape[0], outs), jnp.float32),
            pltpu.SemaphoreType.DMA((4,)),
            pltpu.SemaphoreType.DMA((7,)),
        ]
        + [pltpu.SemaphoreType.DMA((n,))] * 4
        + [pltpu.SemaphoreType.DMA((bits,))] * 4,
        compiler_params=pltpu.CompilerParams(
            collective_id=0, has_side_effects=True, vmem_limit_bytes=56 * 2**20
        ),
        cost_estimate=pl.CostEstimate(flops=work, bytes_accessed=2**25, transcendentals=0),
    )(x, y, down, up, tokens, value, tags, spill_tags)


def owner_task(rows, tags, first_slot, down, up):
    columns = lax.broadcasted_iota(jnp.int32, (1, down.shape[1]), 1) // ADAPTER_RANK
    mask = (tags.reshape(-1, 1) - 1 - first_slot) == columns
    part = jnp.dot(rows, down, preferred_element_type=jnp.float32)
    part = jnp.where(mask, part, 0.0)
    if lax.axis_size("tensor") > 1:
        folded = jnp.sum(part.reshape(part.shape[0], -1, ADAPTER_RANK), axis=1)
        folded = lax.psum(folded, "tensor")
        part = jnp.where(mask, jnp.tile(folded, (1, down.shape[1] // ADAPTER_RANK)), 0.0)
    return jnp.dot(
        part.astype(jnp.bfloat16), up, preferred_element_type=jnp.float32
    ).astype(jnp.bfloat16)


def plan(row_adapter_index, placement, groups, resident, shares):
    rows = row_adapter_index.shape[0]
    adapters = jnp.arange(placement.shape[0], dtype=jnp.int32)
    slots = jnp.sum(
        jnp.where(row_adapter_index[:, None] == adapters[None, :], placement[None, :], 0), axis=1
    )
    owners = slots // resident
    onehot = owners[:, None] == jnp.arange(groups, dtype=jnp.int32)[None, :]
    order = jnp.arange(rows, dtype=jnp.int32)
    before = (order[:, None] > order[None, :]).astype(jnp.bfloat16)
    ranks = jnp.dot(before, onehot.astype(jnp.bfloat16), preferred_element_type=jnp.float32)
    position = jnp.sum(jnp.where(onehot, ranks, 0.0), axis=1).astype(jnp.int32)
    over = jnp.maximum(jnp.sum(onehot.astype(jnp.int32), axis=0) - sum(shares), 0)
    group = jnp.arange(groups, dtype=jnp.int32)
    offset = jnp.sum(jnp.where(group[None, :] < group[:, None], over[None, :], 0), axis=1)
    place = jnp.sum(jnp.where(onehot, offset[None, :], 0), axis=1)
    place = place + position + (groups - 1) * sum(shares)
    end = sum(shares)
    for share in reversed(shares):
        start = end - share
        place = jnp.where(
            position < end, groups * start + owners * share + position - start, place
        )
        end = start
    return slots, place, jnp.sum(over)


def per_device(
    tokens, value_weight, adapter_down_weight, adapter_up_weight, row_adapter_index, placement
):
    rows, width = tokens.shape
    groups, copies = lax.axis_size("dp"), lax.axis_size("rep")
    me = lax.axis_index("dp")
    resident = adapter_down_weight.shape[1] // ADAPTER_RANK
    whole = rows * 5 // (4 * groups)
    fused = lax.axis_size("tensor") == 1 and groups >= 16 and groups & (groups - 1) == 0
    shares = (whole,) if fused else (whole * 3 // 5, whole - whole * 3 // 5)
    spill = rows // 16
    direct = groups * whole
    first_slot = me * resident
    slots, place, over = plan(row_adapter_index, placement, groups, resident, shares)

    def pick(start, count):
        return (start + jnp.arange(count, dtype=jnp.int32))[:, None] == place[None, :]

    def packed(start, count):
        return jnp.dot(
            pick(start, count).astype(jnp.bfloat16), tokens, preferred_element_type=jnp.float32
        ).astype(jnp.bfloat16)

    def tagged(start, count):
        return jnp.sum(jnp.where(pick(start, count), slots[None, :] + 1, 0), axis=1)

    def owned(received, tags):
        return owner_task(received, tags, first_slot, adapter_down_weight, adapter_up_weight)

    def gathered(start):
        return lax.all_gather(packed(start, spill), "dp", tiled=True)

    def scattered(delta):
        return lax.psum_scatter(delta, "dp", scatter_dimension=0, tiled=True)

    def unpacked(start, returned):
        return lax.dot_general(
            pick(start, returned.shape[0]).astype(jnp.bfloat16),
            returned,
            (((0,), (0,)), ((), ())),
            preferred_element_type=jnp.float32,
        )

    starts = (0, groups * shares[0])[: len(shares)]
    notes = jnp.concatenate(
        [tagged(start, groups * share).reshape(groups, share) for start, share in zip(starts, shares)]
        + [
            jnp.broadcast_to(tagged(direct, spill)[None, :], (groups, spill)),
            jnp.broadcast_to(over, (groups, 1)),
        ],
        axis=1,
    )
    notes = lax.all_to_all(jnp.tile(notes, (copies, 1)), ("rep", "dp"), 0, 0, tiled=True)
    most = jnp.max(notes[:, -1])
    notes = lax.dynamic_slice_in_dim(notes, lax.axis_index("rep") * groups, groups, 0)

    if fused:
        bits = groups.bit_length() - 1
        mirror = [mirrored(s, bits) for s in range(groups)]
        local = notes[:, : whole + spill] - 1 - first_slot
        spill_local = jnp.stack([local[s, whole:] for s in mirror])
        back, spill_back, base = exchange(
            packed(0, direct).reshape(groups, whole, width),
            packed(direct, spill),
            adapter_down_weight,
            adapter_up_weight,
            tokens,
            value_weight,
            jnp.broadcast_to(local[:, :whole, None], (groups, whole, 128)),
            jnp.broadcast_to(spill_local[:, :, None], (groups, spill, 128)),
        )
        backs = [back.reshape(direct, -1)]
    else:
        base = lax.psum_scatter(
            jnp.dot(tokens, value_weight, preferred_element_type=jnp.float32),
            "tensor",
            scatter_dimension=1,
            tiled=True,
        )
        spilled = gathered(direct)
        arrived = [
            lax.all_to_all(
                packed(start, groups * share).reshape(groups, share, width), "dp", 0, 0, tiled=True
            ).reshape(groups * share, width)
            for start, share in zip(starts, shares)
        ]
        base, spilled = lax.optimization_barrier((base, spilled))
        spill_back = scattered(owned(spilled, notes[:, whole : whole + spill]))
        backs = []
        for at, share, block in zip((0, shares[0]), shares, arrived):
            delta = owned(block, notes[:, at : at + share])
            backs.append(
                lax.all_to_all(delta.reshape(groups, share, -1), "dp", 0, 0, tiled=True).reshape(
                    groups * share, -1
                )
            )
    row_delta = unpacked(0, jnp.concatenate(backs + [spill_back], axis=0))

    def more(state):
        return state[0] < most

    def again(state):
        done, total = state
        tags = lax.all_gather(tagged(direct + done, spill), "dp", tiled=True)
        back = scattered(owned(gathered(direct + done), tags))
        return done + spill, total + unpacked(direct + done, back)

    row_delta = lax.while_loop(more, again, (jnp.int32(spill), row_delta))[1]
    return (base + row_delta).astype(jnp.bfloat16)


def solution(mesh):
    placed = (
        P(("rep", "dp"), "tensor"),
        P("tensor", None),
        P("tensor", "dp"),
        P("dp", "tensor"),
        P(("rep", "dp")),
        P("rep"),
    )
    return jax.shard_map(
        per_device,
        mesh=mesh,
        in_specs=placed,
        out_specs=P(("rep", "dp"), "tensor"),
        check_vma=False,
    )
```
